512 devices in a mesh: row: 16 (over z), col: 32 (over y, x, core).
Axes of the slice: x: 4, y: 4, z: 16, core: 2. Of those that a mesh axis runs over, the one named last changes fastest.
Arguments:
- left_rows: float32 [2, 2048, 65536], P(None, 'row', 'col'), may hold values from -0.0234375 to 0.0234375
- prior_solution: float32 [65536, 128], P('col'), may hold values from -6 to 6
- diag_rhs: float32 [2, 2048, 128], P(None, 'row'), may hold values from -6 to 6
- inverse_blocks: float32 [2, 2048, 2048], P(None, 'col', 'row'), may hold values from -0.125 to 0.125
- sub_block_t: float32 [2048, 2048], P('col', 'row'), may hold values from -0.125 to 0.125
- trail_panel_t: float32 [2, 2048, 16384], P(None, 'col', 'row'), may hold values from -0.09375 to 0.09375
- trail_rhs: float32 [16384, 128], P(('row', 'col')), may hold values from -6 to 6
Outputs:
- solved: float32 [2, 2048, 128], P(None, 'col')
- trail_out: float32 [16384, 128], P(('row', 'col'))
The draws below stay inside these ranges and needn't reach their ends.
All inputs are finite; a program needn't handle non-finite values.
Results may differ from the reference program's by a relative error of at most 0.000082.
Values sent between devices are 32-bit elements; how exact they have to be, the bound alone decides.
A program may use at most 64 MiB of HBM per device.

```python
import jax
import jax.numpy as jnp
from jax import lax

NB = 2048
NRHS = 128
J = 65536
TR = 16384


def shard_levels(key, dims, cuts, smallest, high):
    def one(axis_at, parts):
        steps = jax.random.uniform(jax.random.fold_in(jax.random.fold_in(key, 6), axis_at), (parts,), jnp.float32, smallest / len(cuts), high / len(cuts))
        return jnp.repeat(jnp.exp(steps), dims[axis_at] // parts).reshape((-1,) + (1,) * (len(dims) - axis_at - 1))

    factor_of = one(*cuts[0])
    for cut in cuts[1:]:
        factor_of = factor_of * one(*cut)
    return factor_of


def noise(stream_key, shape, width, bound, split=(), dtype=jnp.bfloat16):
    result = width * jax.random.normal(stream_key, shape, jnp.float32)
    if split:
        result = result * shard_levels(stream_key, shape, split, -0.22, 0.18)
    return jnp.clip(result, -bound, bound).astype(dtype)


def setup_inputs(seed: int = 0) -> dict:
    arg_keys = jax.random.split(jax.random.key(seed), 8)
    return {
        "left_rows": noise(arg_keys[0], (2, NB, J), J ** -0.5, 0.0234375, ((1, 16), (2, 32)), jnp.float32),
        "prior_solution": noise(arg_keys[1], (J, NRHS), 1.0, 6.0, ((0, 32),), jnp.float32),
        "diag_rhs": noise(arg_keys[2], (2, NB, NRHS), 1.0, 6.0, ((1, 16),), jnp.float32),
        "inverse_blocks": noise(arg_keys[3], (2, NB, NB), NB ** -0.5, 0.125, ((1, 32), (2, 16)), jnp.float32),
        "sub_block_t": noise(arg_keys[4], (NB, NB), NB ** -0.5, 0.125, ((0, 32), (1, 16)), jnp.float32),
        "trail_panel_t": noise(arg_keys[5], (2, NB, TR), (2 * NB) ** -0.5, 0.09375, ((1, 32), (2, 16)), jnp.float32),
        "trail_rhs": noise(arg_keys[6], (TR, NRHS), 1.0, 6.0, ((0, 512),), jnp.float32),
    }


def reference(left_rows, prior_solution, diag_rhs, inverse_blocks, sub_block_t, trail_panel_t, trail_rhs):
    precise = lax.Precision.HIGHEST
    products = jnp.einsum("knj,jr->knr", left_rows, prior_solution, precision=precise)
    residue = diag_rhs - products
    lower_first = jnp.tril(inverse_blocks[0])
    lower_second = jnp.tril(inverse_blocks[1])
    first = jnp.dot(lower_first, residue[0], precision=precise)
    update = jnp.dot(sub_block_t.T, first, precision=precise)
    second = jnp.dot(lower_second, residue[1] - update, precision=precise)
    solved = jnp.stack([first, second])
    trail_sum = jnp.einsum("knt,knr->tr", trail_panel_t, solved, precision=precise)
    return solved, trail_rhs - trail_sum
```

```python
import jax
import jax.numpy as jnp
from jax import lax
from jax.experimental import pallas as pl
from jax.experimental.pallas import tpu as pltpu
from jax.sharding import PartitionSpec as P


F32 = jnp.float32
BF16 = jnp.bfloat16
MESH = pl.DeviceIdType.MESH
NZ = 16
CHUNKS = 4
WINDOW = 8


def ring4(d):
    return min(d, 4 - d)


CHIPS = sorted(((dy, dx) for dy in range(4) for dx in range(4)), key=lambda o: (-(ring4(o[0]) + ring4(o[1])), o))
FAR_Z = sorted(range(1, NZ), key=lambda d: -min(d, NZ - d))


def split(x):
    high = x.astype(BF16)
    return high, (x - high.astype(F32)).astype(BF16)


def dot(a, b):
    return jnp.dot(a, b, preferred_element_type=F32)


def tree_sum(terms):
    terms = list(terms)
    while len(terms) > 1:
        paired = [terms[i] + terms[i + 1] for i in range(0, len(terms) - 1, 2)]
        if len(terms) % 2:
            paired.append(terms[-1])
        terms = paired
    return terms[0]


def kernel(
    left, prior, diag, inverse, sub, panel, rhs, solved_ref, out_ref,
    left_v, prior_v, diag_v, inverse_v, sub_g, low_g, panel_v, rhs_v,
    prior_w, diag_t, part0, part1, red0, red1, res0, res1, res1_in, low0_h, low0_l,
    first_s, first_z, first_g, sub_h, sub_l, upd_s, upd_r, x_t, low1_w, second_z,
    panel_w, sib_s, sib_r, trail_s, trail_r,
    load_sem, chunk_sem, send_sem, recv_sem, sib_sem,
):
    r = lax.axis_index("row")
    c = lax.axis_index("col")
    y, x, k = c // 8, (c // 2) % 4, c % 2
    q = c // 2
    ys = [(y + d) % 4 for d in range(4)]
    xs = [(x + d) % 4 for d in range(4)]
    zs = [(r + d) % NZ for d in range(NZ)]

    def chip(o):
        return ys[o[0]] * 4 + xs[o[1]]

    src_row = (r + NZ - 4 + q // 2) % NZ
    src_chip = 2 * (r % 8) + q % 2
    ahead = (r - q // 2 + 4 + NZ) % NZ
    dst_row = q // 2 + 8 * (ahead // 8)
    dst_chip = 2 * (ahead % 8) + q % 2
    away = jnp.logical_or(dst_row != r, dst_chip != q)

    step = prior.shape[0] // CHUNKS
    for i in range(CHUNKS):
        rows = pl.ds(i * step, step)
        pltpu.make_async_copy(prior.at[rows, :], prior_v.at[rows, :], chunk_sem.at[0, i]).start()
        pltpu.make_async_copy(left.at[0, :, rows], left_v.at[0, :, rows], chunk_sem.at[1, i]).start()
    loads = [
        pltpu.make_async_copy(left.at[1], left_v.at[1], load_sem.at[0]),
        pltpu.make_async_copy(diag.at[k], diag_v, load_sem.at[1]),
        pltpu.make_async_copy(inverse, inverse_v, load_sem.at[2]),
        pltpu.make_async_copy(sub, sub_g.at[4], load_sem.at[3]),
        pltpu.make_async_copy(panel, panel_v, load_sem.at[4]),
        pltpu.make_async_copy(rhs, rhs_v, load_sem.at[5]),
    ]
    for copy in loads:
        copy.start()

    barrier = pltpu.get_barrier_semaphore()

    def greet(row, col):
        pl.semaphore_signal(barrier, inc=1, device_id=(row, col), device_id_type=MESH)

    for d in FAR_Z:
        greet(zs[d], c)
    for o in CHIPS:
        greet(r, 2 * chip(o) + (1 - k))
        if o != (0, 0):
            greet(r, 2 * chip(o) + k)

    @pl.when(jnp.logical_and(k == 1, away))
    def _():
        greet(src_row, 2 * src_chip + 1)

    def remote(src, dst, number, row, col):
        pltpu.make_async_remote_copy(
            src_ref=src, dst_ref=dst, send_sem=send_sem.at[number], recv_sem=recv_sem.at[number],
            device_id=(row, col), device_id_type=MESH,
        ).start()

    def received(ref, number):
        pltpu.make_async_copy(ref, ref, recv_sem.at[number]).wait()

    def sent(ref, number):
        pltpu.make_async_copy(ref, ref, send_sem.at[number]).wait()

    def to_reducers(src, dst, core, number):
        for o in CHIPS[:-1]:
            remote(src.at[chip(o)], dst.at[2 * (4 * o[0] + o[1]) + k], number, r, 2 * chip(o) + core)

        @pl.when(k != core)
        def _():
            remote(src.at[q], dst.at[k], number, r, 2 * q + core)

        @pl.when(k == core)
        def _():
            dst[core] = src[q]

    def to_reducers_sent(ref, core, number):
        @pl.when(k == core)
        def _():
            sent(ref.at[pl.ds(0, 15)], number)

        @pl.when(k != core)
        def _():
            sent(ref, number)

    def from_reducer(ref, core, number):
        for o in CHIPS:
            remote(ref.at[q], ref.at[q], number, r, 2 * chip(o) + (1 - core))
            if o != (0, 0):
                remote(ref.at[q], ref.at[q], number, r, 2 * chip(o) + core)

    def from_reducers_received(ref, core, number):
        @pl.when(k == core)
        def _():
            received(ref.at[pl.ds(0, 15)], number)

        @pl.when(k != core)
        def _():
            received(ref, number)

    def window(ref, slot, number):
        for w in (0, 1, 7, 2, 6, 3, 5):
            to = slot(w)
            remote(ref.at[slot(4)], ref.at[to], number, zs[(4 - w) % NZ], c)

    def left_product(b, parts):
        total = None
        for i in parts:
            rows = pl.ds(i * step, step)
            if b == 0:
                pltpu.make_async_copy(prior.at[rows, :], prior_v.at[rows, :], chunk_sem.at[0, i]).wait()
                prior_w[rows, :] = jnp.concatenate(split(prior_v[rows, :]), axis=1)
                pltpu.make_async_copy(left.at[0, :, rows], left_v.at[0, :, rows], chunk_sem.at[1, i]).wait()
            high, low = split(left_v[b, :, rows])
            wide = dot(high, prior_w[rows, :])
            term = wide[:, :128] + wide[:, 128:] + dot(low, prior_w[rows, :128])
            total = term if total is None else total + term
        return total.T.reshape(16, 8, 128)

    part0[...] = left_product(0, range(CHUNKS))

    pl.semaphore_wait(barrier, 46 + jnp.where(jnp.logical_and(k == 1, away), 1, 0))

    to_reducers(part0, red0, 0, 0)

    loads[3].wait()
    window(sub_g, lambda w: w, 4)

    loads[0].wait()
    part1[...] = left_product(1, range(CHUNKS))
    to_reducers(part1, red1, 1, 1)

    loads[1].wait()
    diag_t[...] = diag_v[...].T.reshape(16, 8, 128)
    loads[2].wait()
    row_ids = c * 64 + lax.broadcasted_iota(jnp.int32, (64, 128), 0)
    col_ids = r * 128 + lax.broadcasted_iota(jnp.int32, (64, 128), 1)
    keep = row_ids >= col_ids
    low0 = jnp.where(keep, inverse_v[0], 0.0)
    nothing = jnp.zeros((64, 128), F32)
    high, low = split(
        jnp.concatenate(
            [jnp.concatenate([low0, nothing], axis=1), jnp.concatenate([nothing, low0], axis=1)], axis=0
        ).T
    )
    low0_h[...] = high
    low0_l[...] = low
    low_g[4] = jnp.where(keep, inverse_v[1], 0.0)

    @pl.when(k == 0)
    def _():
        received(red0.at[pl.ds(0, 31)], 0)
        res0[q] = diag_t[q] - tree_sum(red0[i] for i in range(32))
        from_reducer(res0, 0, 2)

    @pl.when(k == 1)
    def _():
        received(red1.at[pl.ds(0, 31)], 1)
        mine = diag_t[q] - tree_sum(red1[i] for i in range(32))

        @pl.when(away)
        def _():
            res1[...] = mine
            remote(res1, res1_in, 3, dst_row, 2 * dst_chip + 1)

        @pl.when(jnp.logical_not(away))
        def _():
            res1_in[...] = mine

    to_reducers_sent(part0, 0, 0)
    to_reducers_sent(part1, 1, 1)
    from_reducers_received(res0, 0, 2)

    even = jnp.concatenate([res0[2 * i] for i in range(8)], axis=0)
    odd = jnp.concatenate([res0[2 * i + 1] for i in range(8)], axis=0)
    high, low = split(jnp.concatenate([even, odd], axis=1))
    both = dot(jnp.concatenate([high, low], axis=0), low0_h[...])
    first_s[...] = (both[:64] + both[64:] + dot(high, low0_l[...])).reshape(8, 8, 128)
    for d in FAR_Z:
        remote(first_s.at[zs[d] % 8], first_z.at[d], 5, zs[d], c)
    window(low_g, lambda w: w, 6)
    group = r % 8

    loads[4].wait()
    for i in range(8):
        block = panel_v[:, :, 128 * i:128 * (i + 1)].reshape(128, 128).T
        panel_w[4 * i:4 * (i + 1)] = jnp.concatenate(split(block), axis=1).reshape(4, 32, 256)
    received(sub_g.at[pl.ds(0, 7)], 4)
    for w in range(WINDOW):
        high, low = split(sub_g[w])
        sub_h[:, 128 * w:128 * (w + 1)] = high
        sub_l[:, 128 * w:128 * (w + 1)] = low

    @pl.when(k == 0)
    def _():
        sent(red0.at[pl.ds(0, 31)], 2)

    @pl.when(jnp.logical_and(k == 1, away))
    def _():
        sent(res1, 3)
        received(res1_in, 3)

    received(first_z.at[pl.ds(0, 15)], 5)
    first = first_s[group] + tree_sum(first_z[d] for d in range(1, NZ))
    first_g[group] = first

    high, low = split(jnp.concatenate([first[:, :64], first[:, 64:]], axis=0))
    both = dot(jnp.concatenate([high, low], axis=0), sub_h[...])
    update = both[:16] + both[16:] + dot(high, sub_l[...])
    for w in range(WINDOW):
        for h in range(2):
            upd_s[2 * w + h] = update[8 * h:8 * (h + 1), 128 * w:128 * (w + 1)]
    to_reducers(upd_s, upd_r, 1, 7)

    for w in (0, 1, 7, 2, 6, 3, 5):
        remote(first_g.at[group], first_g.at[group], 8, zs[(4 - w) % NZ], c)
    sent(first_z.at[pl.ds(0, 15)], 5)
    sent(sub_g.at[pl.ds(0, 7)], 4)

    @pl.when(k == 1)
    def _():
        received(upd_r.at[pl.ds(0, 31)], 7)
        x_t[q] = res1_in[...] - tree_sum(upd_r[i] for i in range(32))
        from_reducer(x_t, 1, 9)

    received(low_g.at[pl.ds(0, 7)], 6)
    for w in range(WINDOW):
        high, low = split(low_g[w])
        stacked = jnp.concatenate([high.astype(F32), low.astype(F32)], axis=0).T
        low1_w[128 * w:128 * (w + 1), :] = stacked.astype(BF16)
    to_reducers_sent(upd_s, 1, 7)
    sent(low_g.at[pl.ds(0, 7)], 6)
    received(first_g.at[pl.ds(0, 7)], 8)
    sent(first_g.at[pl.ds(0, 7)], 8)
    from_reducers_received(x_t, 1, 9)

    upper = jnp.concatenate([x_t[2 * w] for w in range(WINDOW)], axis=1)
    under = jnp.concatenate([x_t[2 * w + 1] for w in range(WINDOW)], axis=1)
    high, low = split(jnp.concatenate([upper, under], axis=0))
    both = dot(jnp.concatenate([high, low], axis=0), low1_w[...])
    both = both[:16] + both[16:]
    both = both + pltpu.roll(both, 64, 1)
    left_half = lax.broadcasted_iota(jnp.int32, (8, 128), 1) < 64
    second_z[r] = jnp.where(left_half, both[:8], both[8:])
    for d in FAR_Z:
        remote(second_z.at[r], second_z.at[r], 10, zs[d], c)

    @pl.when(k == 1)
    def _():
        sent(upd_r.at[pl.ds(0, 31)], 9)

    received(second_z.at[pl.ds(0, 15)], 10)
    rows = []
    for g in range(8):
        a = first_g[g]
        b = second_z[g] + second_z[g + 8]
        rows.append(jnp.where(left_half, a, pltpu.roll(b, 64, 1)))
        rows.append(jnp.where(left_half, pltpu.roll(a, 64, 1), b))
    solved = jnp.concatenate(rows, axis=0).T
    solved_ref[...] = solved.reshape(2, 64, 128)

    high, low = split(solved)
    weights = jnp.concatenate(
        [jnp.concatenate([high, low], axis=1), jnp.concatenate([high, jnp.zeros((128, 128), BF16)], axis=1)], axis=0
    )

    def trail(group, core):
        lines = jnp.concatenate([panel_w[2 * chip(o) + core] for o in group], axis=0)
        wide = dot(lines, weights)
        return wide[:, :128] + wide[:, 128:]

    groups = [CHIPS[4 * i:4 * (i + 1)] for i in range(4)]
    for i, group in enumerate(groups):
        sib_s[i] = trail(group, 1 - k)
        pltpu.make_async_remote_copy(
            src_ref=sib_s.at[i], dst_ref=sib_r.at[i], send_sem=send_sem.at[11], recv_sem=sib_sem.at[i],
            device_id=(r, 2 * q + (1 - k)), device_id_type=MESH,
        ).start()
    for i, group in enumerate(groups):
        mine = trail(group, k)
        pltpu.make_async_copy(sib_r.at[i], sib_r.at[i], sib_sem.at[i]).wait()
        mine = mine + sib_r[i]
        for j, o in enumerate(group):
            slot = 4 * o[0] + o[1]
            if slot:
                trail_s[slot] = mine[32 * j:32 * (j + 1)]
                remote(trail_s.at[slot], trail_r.at[slot], 12, r, 2 * chip(o) + k)
            else:
                trail_r[0] = mine[32 * j:32 * (j + 1)]
    sent(second_z.at[pl.ds(0, 15)], 10)
    sent(sib_s, 11)
    loads[5].wait()
    received(trail_r.at[pl.ds(0, 15)], 12)
    out_ref[...] = rhs_v[...] - tree_sum(trail_r[i] for i in range(16))
    sent(trail_s.at[pl.ds(0, 15)], 12)


def on_device(*args):
    left, prior, diag, inverse, sub, panel, rhs = args
    tiles = lambda n: pltpu.VMEM((n, 8, 128), F32)
    return pl.pallas_call(
        kernel,
        out_shape=(
            jax.ShapeDtypeStruct((2, 64, 128), F32),
            jax.ShapeDtypeStruct((32, 128), F32),
        ),
        in_specs=[pl.BlockSpec(memory_space=pl.ANY)] * 7,
        out_specs=(pl.BlockSpec(memory_space=pltpu.VMEM), pl.BlockSpec(memory_space=pltpu.VMEM)),
        scratch_shapes=[
            pltpu.VMEM((2, 128, 2048), F32),
            pltpu.VMEM((2048, 128), F32),
            pltpu.VMEM((128, 128), F32),
            pltpu.VMEM((2, 64, 128), F32),
            pltpu.VMEM((WINDOW, 64, 128), F32),
            pltpu.VMEM((WINDOW, 64, 128), F32),
            pltpu.VMEM((2, 64, 1024), F32),
            pltpu.VMEM((32, 128), F32),
            pltpu.VMEM((2048, 256), BF16),
            tiles(16),
            tiles(16),
            tiles(16),
            tiles(32),
            tiles(32),
            tiles(16),
            pltpu.VMEM((8, 128), F32),
            pltpu.VMEM((8, 128), F32),
            pltpu.VMEM((256, 128), BF16),
            pltpu.VMEM((256, 128), BF16),
            tiles(8),
            tiles(16),
            tiles(8),
            pltpu.VMEM((64, 1024), BF16),
            pltpu.VMEM((64, 1024), BF16),
            tiles(16),
            tiles(32),
            tiles(16),
            pltpu.VMEM((1024, 128), BF16),
            tiles(16),
            pltpu.VMEM((32, 32, 256), BF16),
            pltpu.VMEM((4, 128, 128), F32),
            pltpu.VMEM((4, 128, 128), F32),
            pltpu.VMEM((16, 32, 128), F32),
            pltpu.VMEM((16, 32, 128), F32),
            pltpu.SemaphoreType.DMA((6,)),
            pltpu.SemaphoreType.DMA((2, CHUNKS)),
            pltpu.SemaphoreType.DMA((13,)),
            pltpu.SemaphoreType.DMA((13,)),
            pltpu.SemaphoreType.DMA((4,)),
        ],
        compiler_params=pltpu.CompilerParams(
            collective_id=0, has_side_effects=True, vmem_limit_bytes=48 * 1024 * 1024
        ),
    )(left, prior, diag, inverse, sub, panel, rhs)


def solution(mesh):
    in_specs = (
        P(None, "row", "col"),
        P("col", None),
        P(None, "row", None),
        P(None, "col", "row"),
        P("col", "row"),
        P(None, "col", "row"),
        P(("row", "col"), None),
    )
    out_specs = (P(None, "col", None), P(("row", "col"), None))
    return jax.shard_map(
        on_device, mesh=mesh, in_specs=in_specs, out_specs=out_specs, check_vma=False
    )
```

```python
import jax
import jax.numpy as jnp
from jax import lax
from jax.experimental import pallas as pl
from jax.experimental.pallas import tpu as pltpu
from jax.sharding import PartitionSpec as P


F32 = jnp.float32
BF16 = jnp.bfloat16
MESH = pl.DeviceIdType.MESH
NZ = 16
CHUNKS = 4
WINDOW = 8


def ring4(d):
    return min(d, 4 - d)


CHIPS = sorted(((dy, dx) for dy in range(4) for dx in range(4)), key=lambda o: (-(ring4(o[0]) + ring4(o[1])), o))
NEAR_Z = (4, 12, 3, 13, 2, 14, 1, 15)
FAR_Z = sorted(range(1, NZ), key=lambda d: -min(d, NZ - d))


def split(x):
    high = x.astype(BF16)
    return high, (x - high.astype(F32)).astype(BF16)


def dot(a, b):
    return jnp.dot(a, b, preferred_element_type=F32)


def tree_sum(terms):
    terms = list(terms)
    while len(terms) > 1:
        paired = [terms[i] + terms[i + 1] for i in range(0, len(terms) - 1, 2)]
        if len(terms) % 2:
            paired.append(terms[-1])
        terms = paired
    return terms[0]


def kernel(
    left, prior, diag, inverse, sub, panel, rhs, solved_ref, out_ref,
    left_v, prior_v, diag_v, inverse_v, sub_g, low_g, panel_v, rhs_v,
    prior_w, diag_t, part0, part1, red0, red1, res0, res1, res1_in, low0_h, low0_l,
    first_s, first_z, first_g, sub_h, sub_l, upd_s, upd_r, x_t, low1_w, second_z,
    panel_w, sib_s, sib_r, trail_s, trail_r,
    load_sem, chunk_sem, send_sem, recv_sem, sib_sem, passed_sem,
):
    r = lax.axis_index("row")
    c = lax.axis_index("col")
    y, x, k = c // 8, (c // 2) % 4, c % 2
    q = c // 2
    ys = [(y + d) % 4 for d in range(4)]
    xs = [(x + d) % 4 for d in range(4)]
    zs = [(r + d) % NZ for d in range(NZ)]

    def chip(o):
        return ys[o[0]] * 4 + xs[o[1]]

    ahead = (r - q // 2 + 4 + NZ) % NZ
    dst_row = q // 2 + 8 * (ahead // 8)
    dst_chip = 2 * (ahead % 8) + q % 2
    away = jnp.logical_or(dst_row != r, dst_chip != q)

    step = prior.shape[0] // CHUNKS
    for i in range(CHUNKS):
        rows = pl.ds(i * step, step)
        pltpu.make_async_copy(prior.at[rows, :], prior_v.at[rows, :], chunk_sem.at[0, i]).start()
        pltpu.make_async_copy(left.at[0, :, rows], left_v.at[0, :, rows], chunk_sem.at[1, i]).start()
    loads = [
        pltpu.make_async_copy(left.at[1], left_v.at[1], load_sem.at[0]),
        pltpu.make_async_copy(diag.at[k], diag_v, load_sem.at[1]),
        pltpu.make_async_copy(inverse, inverse_v, load_sem.at[2]),
        pltpu.make_async_copy(sub, sub_g.at[4], load_sem.at[3]),
        pltpu.make_async_copy(panel, panel_v, load_sem.at[4]),
        pltpu.make_async_copy(rhs, rhs_v, load_sem.at[5]),
    ]

    barrier = pltpu.get_barrier_semaphore()

    def greet(row, col):
        pl.semaphore_signal(barrier, inc=1, device_id=(row, col), device_id_type=MESH)

    for o in CHIPS[:5]:
        greet(r, 2 * chip(o) + (1 - k))
        greet(r, 2 * chip(o) + k)
    for d in NEAR_Z:
        greet(zs[d], c)
    for o in CHIPS[5:]:
        greet(r, 2 * chip(o) + (1 - k))
        if o != (0, 0):
            greet(r, 2 * chip(o) + k)
    for copy in loads:
        copy.start()

    def remote(src, dst, number, row, col):
        pltpu.make_async_remote_copy(
            src_ref=src, dst_ref=dst, send_sem=send_sem.at[number], recv_sem=recv_sem.at[number],
            device_id=(row, col), device_id_type=MESH,
        ).start()

    def received(ref, number):
        pltpu.make_async_copy(ref, ref, recv_sem.at[number]).wait()

    def sent(ref, number):
        pltpu.make_async_copy(ref, ref, send_sem.at[number]).wait()

    def to_reducers(src, dst, core, number):
        for o in CHIPS[:-1]:
            remote(src.at[chip(o)], dst.at[2 * (4 * o[0] + o[1]) + k], number, r, 2 * chip(o) + core)

        @pl.when(k != core)
        def _():
            remote(src.at[q], dst.at[k], number, r, 2 * q + core)

        @pl.when(k == core)
        def _():
            dst[core] = src[q]

    def to_reducers_sent(ref, core, number):
        @pl.when(k == core)
        def _():
            sent(ref.at[pl.ds(0, 15)], number)

        @pl.when(k != core)
        def _():
            sent(ref, number)

    def from_reducer(ref, core, number):
        for o in CHIPS:
            remote(ref.at[q], ref.at[q], number, r, 2 * chip(o) + (1 - core))
            if o != (0, 0):
                remote(ref.at[q], ref.at[q], number, r, 2 * chip(o) + core)

    def from_reducers_received(ref, core, number):
        @pl.when(k == core)
        def _():
            received(ref.at[pl.ds(0, 15)], number)

        @pl.when(k != core)
        def _():
            received(ref, number)

    def window(ref, slot, number):
        for w in (0, 1, 7, 2, 6, 3, 5):
            to = slot(w)
            remote(ref.at[slot(4)], ref.at[to], number, zs[(4 - w) % NZ], c)

    def left_product(b, parts):
        total = None
        for i in parts:
            rows = pl.ds(i * step, step)
            if b == 0:
                pltpu.make_async_copy(prior.at[rows, :], prior_v.at[rows, :], chunk_sem.at[0, i]).wait()
                prior_w[rows, :] = jnp.concatenate(split(prior_v[rows, :]), axis=1)
                pltpu.make_async_copy(left.at[0, :, rows], left_v.at[0, :, rows], chunk_sem.at[1, i]).wait()
            high, low = split(left_v[b, :, rows])
            wide = dot(high, prior_w[rows, :])
            term = wide[:, :128] + wide[:, 128:] + dot(low, prior_w[rows, :128])
            total = term if total is None else total + term
        return total.T.reshape(16, 8, 128)

    part0[...] = left_product(0, range(CHUNKS))

    pl.semaphore_wait(barrier, 39)

    to_reducers(part0, red0, 0, 0)
    for d in NEAR_Z:
        pl.semaphore_signal(passed_sem, inc=1, device_id=(zs[d], c), device_id_type=MESH)

    loads[3].wait()
    window(sub_g, lambda w: w, 4)

    loads[1].wait()
    diag_t[...] = diag_v[...].T.reshape(16, 8, 128)
    loads[2].wait()
    row_ids = c * 64 + lax.broadcasted_iota(jnp.int32, (64, 128), 0)
    col_ids = r * 128 + lax.broadcasted_iota(jnp.int32, (64, 128), 1)
    keep = row_ids >= col_ids
    low0 = jnp.where(keep, inverse_v[0], 0.0)
    nothing = jnp.zeros((64, 128), F32)
    high, low = split(
        jnp.concatenate(
            [jnp.concatenate([low0, nothing], axis=1), jnp.concatenate([nothing, low0], axis=1)], axis=0
        ).T
    )
    low0_h[...] = high
    low0_l[...] = low
    low_g[4] = jnp.where(keep, inverse_v[1], 0.0)

    @pl.when(k == 0)
    def _():
        received(red0.at[pl.ds(0, 31)], 0)
        res0[q] = diag_t[q] - tree_sum(red0[i] for i in range(32))
        from_reducer(res0, 0, 2)

    loads[0].wait()
    part1[...] = left_product(1, range(CHUNKS))
    to_reducers(part1, red1, 1, 1)
    to_reducers_sent(part0, 0, 0)
    from_reducers_received(res0, 0, 2)

    even = jnp.concatenate([res0[2 * i] for i in range(8)], axis=0)
    odd = jnp.concatenate([res0[2 * i + 1] for i in range(8)], axis=0)
    high, low = split(jnp.concatenate([even, odd], axis=1))
    both = dot(jnp.concatenate([high, low], axis=0), low0_h[...])
    first_s[...] = (both[:64] + both[64:] + dot(high, low0_l[...])).reshape(8, 8, 128)
    pl.semaphore_wait(passed_sem, 8)
    for d in FAR_Z:
        remote(first_s.at[zs[d] % 8], first_z.at[d], 5, zs[d], c)
    window(low_g, lambda w: w, 6)
    group = r % 8

    @pl.when(k == 1)
    def _():
        received(red1.at[pl.ds(0, 31)], 1)
        mine = diag_t[q] - tree_sum(red1[i] for i in range(32))

        @pl.when(away)
        def _():
            res1[...] = mine
            remote(res1, res1_in, 3, dst_row, 2 * dst_chip + 1)

        @pl.when(jnp.logical_not(away))
        def _():
            res1_in[...] = mine

    to_reducers_sent(part1, 1, 1)
    loads[4].wait()
    for i in range(8):
        block = panel_v[:, :, 128 * i:128 * (i + 1)].reshape(128, 128).T
        panel_w[4 * i:4 * (i + 1)] = jnp.concatenate(split(block), axis=1).reshape(4, 32, 256)
    received(sub_g.at[pl.ds(0, 7)], 4)
    for w in range(WINDOW):
        high, low = split(sub_g[w])
        sub_h[:, 128 * w:128 * (w + 1)] = high
        sub_l[:, 128 * w:128 * (w + 1)] = low

    @pl.when(k == 0)
    def _():
        sent(red0.at[pl.ds(0, 31)], 2)

    @pl.when(jnp.logical_and(k == 1, away))
    def _():
        sent(res1, 3)
        received(res1_in, 3)

    received(first_z.at[pl.ds(0, 15)], 5)
    first = first_s[group] + tree_sum(first_z[d] for d in range(1, NZ))
    first_g[group] = first

    high, low = split(jnp.concatenate([first[:, :64], first[:, 64:]], axis=0))
    both = dot(jnp.concatenate([high, low], axis=0), sub_h[...])
    update = both[:16] + both[16:] + dot(high, sub_l[...])
    for w in range(WINDOW):
        for h in range(2):
            upd_s[2 * w + h] = update[8 * h:8 * (h + 1), 128 * w:128 * (w + 1)]
    to_reducers(upd_s, upd_r, 1, 7)

    for w in (0, 1, 7, 2, 6, 3, 5):
        remote(first_g.at[group], first_g.at[group], 8, zs[(4 - w) % NZ], c)
    sent(first_z.at[pl.ds(0, 15)], 5)
    sent(sub_g.at[pl.ds(0, 7)], 4)

    @pl.when(k == 1)
    def _():
        received(upd_r.at[pl.ds(0, 31)], 7)
        x_t[q] = res1_in[...] - tree_sum(upd_r[i] for i in range(32))
        from_reducer(x_t, 1, 9)

    received(low_g.at[pl.ds(0, 7)], 6)
    for w in range(WINDOW):
        high, low = split(low_g[w])
        stacked = jnp.concatenate([high.astype(F32), low.astype(F32)], axis=0).T
        low1_w[128 * w:128 * (w + 1), :] = stacked.astype(BF16)
    to_reducers_sent(upd_s, 1, 7)
    sent(low_g.at[pl.ds(0, 7)], 6)
    received(first_g.at[pl.ds(0, 7)], 8)
    sent(first_g.at[pl.ds(0, 7)], 8)
    from_reducers_received(x_t, 1, 9)

    upper = jnp.concatenate([x_t[2 * w] for w in range(WINDOW)], axis=1)
    under = jnp.concatenate([x_t[2 * w + 1] for w in range(WINDOW)], axis=1)
    high, low = split(jnp.concatenate([upper, under], axis=0))
    both = dot(jnp.concatenate([high, low], axis=0), low1_w[...])
    both = both[:16] + both[16:]
    both = both + pltpu.roll(both, 64, 1)
    left_half = lax.broadcasted_iota(jnp.int32, (8, 128), 1) < 64
    second_z[r] = jnp.where(left_half, both[:8], both[8:])
    for d in FAR_Z:
        remote(second_z.at[r], second_z.at[r], 10, zs[d], c)

    @pl.when(k == 1)
    def _():
        sent(upd_r.at[pl.ds(0, 31)], 9)

    received(second_z.at[pl.ds(0, 15)], 10)
    rows = []
    for g in range(8):
        a = first_g[g]
        b = second_z[g] + second_z[g + 8]
        rows.append(jnp.where(left_half, a, pltpu.roll(b, 64, 1)))
        rows.append(jnp.where(left_half, pltpu.roll(a, 64, 1), b))
    solved = jnp.concatenate(rows, axis=0).T
    solved_ref[...] = solved.reshape(2, 64, 128)

    high, low = split(solved)
    weights = jnp.concatenate(
        [jnp.concatenate([high, low], axis=1), jnp.concatenate([high, jnp.zeros((128, 128), BF16)], axis=1)], axis=0
    )

    def trail(group, core):
        lines = jnp.concatenate([panel_w[2 * chip(o) + core] for o in group], axis=0)
        wide = dot(lines, weights)
        return wide[:, :128] + wide[:, 128:]

    groups = [CHIPS[4 * i:4 * (i + 1)] for i in range(4)]
    for i, group in enumerate(groups):
        sib_s[i] = trail(group, 1 - k)
        pltpu.make_async_remote_copy(
            src_ref=sib_s.at[i], dst_ref=sib_r.at[i], send_sem=send_sem.at[11], recv_sem=sib_sem.at[i],
            device_id=(r, 2 * q + (1 - k)), device_id_type=MESH,
        ).start()
    for i, group in enumerate(groups):
        mine = trail(group, k)
        pltpu.make_async_copy(sib_r.at[i], sib_r.at[i], sib_sem.at[i]).wait()
        mine = mine + sib_r[i]
        for j, o in enumerate(group):
            slot = 4 * o[0] + o[1]
            if slot:
                trail_s[slot] = mine[32 * j:32 * (j + 1)]
                remote(trail_s.at[slot], trail_r.at[slot], 12, r, 2 * chip(o) + k)
            else:
                trail_r[0] = mine[32 * j:32 * (j + 1)]
    sent(second_z.at[pl.ds(0, 15)], 10)
    sent(sib_s, 11)
    loads[5].wait()
    received(trail_r.at[pl.ds(0, 15)], 12)
    out_ref[...] = rhs_v[...] - tree_sum(trail_r[i] for i in range(16))
    sent(trail_s.at[pl.ds(0, 15)], 12)


def on_device(*args):
    left, prior, diag, inverse, sub, panel, rhs = args
    tiles = lambda n: pltpu.VMEM((n, 8, 128), F32)
    return pl.pallas_call(
        kernel,
        out_shape=(
            jax.ShapeDtypeStruct((2, 64, 128), F32),
            jax.ShapeDtypeStruct((32, 128), F32),
        ),
        in_specs=[pl.BlockSpec(memory_space=pl.ANY)] * 7,
        out_specs=(pl.BlockSpec(memory_space=pltpu.VMEM), pl.BlockSpec(memory_space=pltpu.VMEM)),
        scratch_shapes=[
            pltpu.VMEM((2, 128, 2048), F32),
            pltpu.VMEM((2048, 128), F32),
            pltpu.VMEM((128, 128), F32),
            pltpu.VMEM((2, 64, 128), F32),
            pltpu.VMEM((WINDOW, 64, 128), F32),
            pltpu.VMEM((WINDOW, 64, 128), F32),
            pltpu.VMEM((2, 64, 1024), F32),
            pltpu.VMEM((32, 128), F32),
            pltpu.VMEM((2048, 256), BF16),
            tiles(16),
            tiles(16),
            tiles(16),
            tiles(32),
            tiles(32),
            tiles(16),
            pltpu.VMEM((8, 128), F32),
            pltpu.VMEM((8, 128), F32),
            pltpu.VMEM((256, 128), BF16),
            pltpu.VMEM((256, 128), BF16),
            tiles(8),
            tiles(16),
            tiles(8),
            pltpu.VMEM((64, 1024), BF16),
            pltpu.VMEM((64, 1024), BF16),
            tiles(16),
            tiles(32),
            tiles(16),
            pltpu.VMEM((1024, 128), BF16),
            tiles(16),
            pltpu.VMEM((32, 32, 256), BF16),
            pltpu.VMEM((4, 128, 128), F32),
            pltpu.VMEM((4, 128, 128), F32),
            pltpu.VMEM((16, 32, 128), F32),
            pltpu.VMEM((16, 32, 128), F32),
            pltpu.SemaphoreType.DMA((6,)),
            pltpu.SemaphoreType.DMA((2, CHUNKS)),
            pltpu.SemaphoreType.DMA((13,)),
            pltpu.SemaphoreType.DMA((13,)),
            pltpu.SemaphoreType.DMA((4,)),
            pltpu.SemaphoreType.REGULAR,
        ],
        compiler_params=pltpu.CompilerParams(
            collective_id=0, has_side_effects=True, vmem_limit_bytes=60 * 1024 * 1024
        ),
    )(left, prior, diag, inverse, sub, panel, rhs)


def solution(mesh):
    in_specs = (
        P(None, "row", "col"),
        P("col", None),
        P(None, "row", None),
        P(None, "col", "row"),
        P("col", "row"),
        P(None, "col", "row"),
        P(("row", "col"), None),
    )
    out_specs = (P(None, "col", None), P(("row", "col"), None))
    return jax.shard_map(
        on_device, mesh=mesh, in_specs=in_specs, out_specs=out_specs, check_vma=False
    )
```

```python
import jax
import jax.numpy as jnp
from jax import lax
from jax.experimental import pallas as pl
from jax.experimental.pallas import tpu as pltpu
from jax.sharding import PartitionSpec as P


F32 = jnp.float32
BF16 = jnp.bfloat16
MESH = pl.DeviceIdType.MESH
NZ = 16
CHUNKS = 4
WINDOW = 8
SUB, LOW = 13, 15


def ring4(d):
    return min(d, 4 - d)


CHIPS = sorted(((dy, dx) for dy in range(4) for dx in range(4)), key=lambda o: (-(ring4(o[0]) + ring4(o[1])), o))
NEAR_Z = (4, 12, 3, 13, 2, 14, 1, 15)
FAR_Z = sorted(range(1, NZ), key=lambda d: -min(d, NZ - d))


def split(x):
    high = x.astype(BF16)
    return high, (x - high.astype(F32)).astype(BF16)


def dot(a, b):
    return jnp.dot(a, b, preferred_element_type=F32)


def tree_sum(terms):
    terms = list(terms)
    while len(terms) > 1:
        paired = [terms[i] + terms[i + 1] for i in range(0, len(terms) - 1, 2)]
        if len(terms) % 2:
            paired.append(terms[-1])
        terms = paired
    return terms[0]


def kernel(
    left, prior, diag, inverse, sub, panel, solved_ref, share_ref,
    left_v, prior_v, diag_v, inverse_v, sub_g, low_g, panel_v,
    prior_w, diag_t, part0, part1, red0, red1, res0, res1, res1_in, low0_h, low0_l,
    first_s, first_z, first_g, sub_h, sub_l, upd_s, upd_r, x_t, low1_w, second_z,
    panel_w, sib_s, sib_r, trail_s, trail_r,
    load_sem, chunk_sem, send_sem, recv_sem, sib_sem, passed_sem,
):
    r = lax.axis_index("row")
    c = lax.axis_index("col")
    y, x, k = c // 8, (c // 2) % 4, c % 2
    q = c // 2
    ys = [(y + d) % 4 for d in range(4)]
    xs = [(x + d) % 4 for d in range(4)]
    zs = [(r + d) % NZ for d in range(NZ)]

    def chip(o):
        return ys[o[0]] * 4 + xs[o[1]]

    ahead = (r - q // 2 + 4 + NZ) % NZ
    dst_row = q // 2 + 8 * (ahead // 8)
    dst_chip = 2 * (ahead % 8) + q % 2
    away = jnp.logical_or(dst_row != r, dst_chip != q)

    step = prior.shape[0] // CHUNKS
    for i in range(CHUNKS):
        rows = pl.ds(i * step, step)
        pltpu.make_async_copy(prior.at[rows, :], prior_v.at[rows, :], chunk_sem.at[0, i]).start()
        pltpu.make_async_copy(left.at[0, :, rows], left_v.at[0, :, rows], chunk_sem.at[1, i]).start()
    loads = [
        pltpu.make_async_copy(left.at[1], left_v.at[1], load_sem.at[0]),
        pltpu.make_async_copy(diag.at[k], diag_v, load_sem.at[1]),
        pltpu.make_async_copy(inverse, inverse_v, load_sem.at[2]),
        pltpu.make_async_copy(sub, sub_g.at[4], load_sem.at[3]),
        pltpu.make_async_copy(panel, panel_v, load_sem.at[4]),
    ]

    barrier = pltpu.get_barrier_semaphore()

    def greet(row, col):
        pl.semaphore_signal(barrier, inc=1, device_id=(row, col), device_id_type=MESH)

    for o in CHIPS[:5]:
        greet(r, 2 * chip(o) + (1 - k))
        greet(r, 2 * chip(o) + k)
    for d in NEAR_Z:
        greet(zs[d], c)
    for o in CHIPS[5:]:
        greet(r, 2 * chip(o) + (1 - k))
        if o != (0, 0):
            greet(r, 2 * chip(o) + k)
    for copy in loads:
        copy.start()

    def remote(src, dst, number, row, col):
        pltpu.make_async_remote_copy(
            src_ref=src, dst_ref=dst, send_sem=send_sem.at[number], recv_sem=recv_sem.at[number],
            device_id=(row, col), device_id_type=MESH,
        ).start()

    def received(ref, number):
        pltpu.make_async_copy(ref, ref, recv_sem.at[number]).wait()

    def sent(ref, number):
        pltpu.make_async_copy(ref, ref, send_sem.at[number]).wait()

    def to_reducers(src, dst, core, number):
        for o in CHIPS[:-1]:
            remote(src.at[chip(o)], dst.at[2 * (4 * o[0] + o[1]) + k], number, r, 2 * chip(o) + core)

        @pl.when(k != core)
        def _():
            remote(src.at[q], dst.at[k], number, r, 2 * q + core)

        @pl.when(k == core)
        def _():
            dst[core] = src[q]

    def to_reducers_sent(ref, core, number):
        @pl.when(k == core)
        def _():
            sent(ref.at[pl.ds(0, 15)], number)

        @pl.when(k != core)
        def _():
            sent(ref, number)

    def from_reducer(ref, core, number):
        for o in CHIPS:
            remote(ref.at[q], ref.at[q], number, r, 2 * chip(o) + (1 - core))
            if o != (0, 0):
                remote(ref.at[q], ref.at[q], number, r, 2 * chip(o) + core)

    def from_reducers_received(ref, core, number):
        @pl.when(k == core)
        def _():
            received(ref.at[pl.ds(0, 15)], number)

        @pl.when(k != core)
        def _():
            received(ref, number)

    def window_start(ref, number):
        for w in (2, 6, 3, 5):
            remote(ref.at[4], ref.at[w], number, zs[(4 - w) % NZ], c)

    def window_hand_on(ref, number):
        received(ref.at[pl.ds(0, 4)], number)
        remote(ref.at[2], ref.at[0], number + 1, zs[2], c)
        remote(ref.at[2], ref.at[1], number + 1, zs[1], c)
        remote(ref.at[6], ref.at[7], number + 1, zs[15], c)

    def window_end(ref, number):
        received(ref.at[pl.ds(0, 3)], number + 1)
        sent(ref.at[pl.ds(0, 4)], number)
        sent(ref.at[pl.ds(0, 3)], number + 1)

    def left_product(b, parts):
        total = None
        for i in parts:
            rows = pl.ds(i * step, step)
            if b == 0:
                pltpu.make_async_copy(prior.at[rows, :], prior_v.at[rows, :], chunk_sem.at[0, i]).wait()
                prior_w[rows, :] = jnp.concatenate(split(prior_v[rows, :]), axis=1)
                pltpu.make_async_copy(left.at[0, :, rows], left_v.at[0, :, rows], chunk_sem.at[1, i]).wait()
            high, low = split(left_v[b, :, rows])
            wide = dot(high, prior_w[rows, :])
            term = wide[:, :128] + wide[:, 128:] + dot(low, prior_w[rows, :128])
            total = term if total is None else total + term
        return total.T.reshape(16, 8, 128)

    part0[...] = left_product(0, range(CHUNKS))

    pl.semaphore_wait(barrier, 39)

    to_reducers(part0, red0, 0, 0)
    for d in NEAR_Z:
        pl.semaphore_signal(passed_sem, inc=1, device_id=(zs[d], c), device_id_type=MESH)

    loads[3].wait()
    window_start(sub_g, SUB)
    loads[2].wait()
    row_ids = c * 64 + lax.broadcasted_iota(jnp.int32, (64, 128), 0)
    col_ids = r * 128 + lax.broadcasted_iota(jnp.int32, (64, 128), 1)
    keep = row_ids >= col_ids
    low_g[4] = jnp.where(keep, inverse_v[1], 0.0)
    window_start(low_g, LOW)
    loads[1].wait()
    diag_t[...] = diag_v[...].T.reshape(16, 8, 128)
    low0 = jnp.where(keep, inverse_v[0], 0.0)
    nothing = jnp.zeros((64, 128), F32)
    high, low = split(
        jnp.concatenate(
            [jnp.concatenate([low0, nothing], axis=1), jnp.concatenate([nothing, low0], axis=1)], axis=0
        ).T
    )
    low0_h[...] = high
    low0_l[...] = low

    loads[0].wait()
    part1[...] = left_product(1, range(CHUNKS))

    @pl.when(k == 0)
    def _():
        received(red0.at[pl.ds(0, 31)], 0)
        res0[q] = diag_t[q] - tree_sum(red0[i] for i in range(32))
        from_reducer(res0, 0, 2)

    to_reducers(part1, red1, 1, 1)
    window_hand_on(sub_g, SUB)
    window_hand_on(low_g, LOW)
    to_reducers_sent(part0, 0, 0)
    from_reducers_received(res0, 0, 2)

    even = jnp.concatenate([res0[2 * i] for i in range(8)], axis=0)
    odd = jnp.concatenate([res0[2 * i + 1] for i in range(8)], axis=0)
    high, low = split(jnp.concatenate([even, odd], axis=1))
    both = dot(jnp.concatenate([high, low], axis=0), low0_h[...])
    first_s[...] = (both[:64] + both[64:] + dot(high, low0_l[...])).reshape(8, 8, 128)
    pl.semaphore_wait(passed_sem, 8)
    for d in FAR_Z:
        remote(first_s.at[zs[d] % 8], first_z.at[d], 5, zs[d], c)
    group = r % 8

    @pl.when(k == 1)
    def _():
        received(red1.at[pl.ds(0, 31)], 1)
        mine = diag_t[q] - tree_sum(red1[i] for i in range(32))

        @pl.when(away)
        def _():
            res1[...] = mine
            remote(res1, res1_in, 3, dst_row, 2 * dst_chip + 1)

        @pl.when(jnp.logical_not(away))
        def _():
            res1_in[...] = mine

    to_reducers_sent(part1, 1, 1)
    loads[4].wait()
    for i in range(8):
        block = panel_v[:, :, 128 * i:128 * (i + 1)].reshape(128, 128).T
        panel_w[4 * i:4 * (i + 1)] = jnp.concatenate(split(block), axis=1).reshape(4, 32, 256)
    window_end(sub_g, SUB)
    for w in range(WINDOW):
        high, low = split(sub_g[w])
        sub_h[:, 128 * w:128 * (w + 1)] = high
        sub_l[:, 128 * w:128 * (w + 1)] = low
    window_end(low_g, LOW)
    for w in range(WINDOW):
        high, low = split(low_g[w])
        stacked = jnp.concatenate([high.astype(F32), low.astype(F32)], axis=0).T
        low1_w[128 * w:128 * (w + 1), :] = stacked.astype(BF16)

    @pl.when(k == 0)
    def _():
        sent(red0.at[pl.ds(0, 31)], 2)

    received(first_z.at[pl.ds(0, 15)], 5)
    first = first_s[group] + tree_sum(first_z[d] for d in range(1, NZ))
    first_g[group] = first

    high, low = split(jnp.concatenate([first[:, :64], first[:, 64:]], axis=0))
    both = dot(jnp.concatenate([high, low], axis=0), sub_h[...])
    update = both[:16] + both[16:] + dot(high, sub_l[...])
    for w in range(WINDOW):
        for h in range(2):
            upd_s[2 * w + h] = update[8 * h:8 * (h + 1), 128 * w:128 * (w + 1)]
    to_reducers(upd_s, upd_r, 1, 7)

    for w in (0, 1, 7, 2, 6, 3, 5):
        remote(first_g.at[group], first_g.at[group], 8, zs[(4 - w) % NZ], c)
    sent(first_z.at[pl.ds(0, 15)], 5)

    @pl.when(k == 1)
    def _():
        @pl.when(away)
        def _():
            sent(res1, 3)
            received(res1_in, 3)

        received(upd_r.at[pl.ds(0, 31)], 7)
        x_t[q] = res1_in[...] - tree_sum(upd_r[i] for i in range(32))
        from_reducer(x_t, 1, 9)

    to_reducers_sent(upd_s, 1, 7)
    received(first_g.at[pl.ds(0, 7)], 8)
    sent(first_g.at[pl.ds(0, 7)], 8)
    from_reducers_received(x_t, 1, 9)

    upper = jnp.concatenate([x_t[2 * w] for w in range(WINDOW)], axis=1)
    under = jnp.concatenate([x_t[2 * w + 1] for w in range(WINDOW)], axis=1)
    high, low = split(jnp.concatenate([upper, under], axis=0))
    both = dot(jnp.concatenate([high, low], axis=0), low1_w[...])
    both = both[:16] + both[16:]
    both = both + pltpu.roll(both, 64, 1)
    left_half = lax.broadcasted_iota(jnp.int32, (8, 128), 1) < 64
    second_z[r] = jnp.where(left_half, both[:8], both[8:])
    for d in FAR_Z:
        remote(second_z.at[r], second_z.at[r], 10, zs[d], c)

    @pl.when(k == 1)
    def _():
        sent(upd_r.at[pl.ds(0, 31)], 9)

    received(second_z.at[pl.ds(0, 15)], 10)
    rows = []
    for g in range(8):
        a = first_g[g]
        b = second_z[g] + second_z[g + 8]
        rows.append(jnp.where(left_half, a, pltpu.roll(b, 64, 1)))
        rows.append(jnp.where(left_half, pltpu.roll(a, 64, 1), b))
    solved = jnp.concatenate(rows, axis=0).T
    solved_ref[...] = solved.reshape(2, 64, 128)

    high, low = split(solved)
    weights = jnp.concatenate(
        [jnp.concatenate([high, low], axis=1), jnp.concatenate([high, jnp.zeros((128, 128), BF16)], axis=1)], axis=0
    )

    def trail(group, core):
        lines = jnp.concatenate([panel_w[2 * chip(o) + core] for o in group], axis=0)
        wide = dot(lines, weights)
        return wide[:, :128] + wide[:, 128:]

    groups = [CHIPS[4 * i:4 * (i + 1)] for i in range(4)]
    for i, group in enumerate(groups):
        sib_s[i] = trail(group, 1 - k)
        pltpu.make_async_remote_copy(
            src_ref=sib_s.at[i], dst_ref=sib_r.at[i], send_sem=send_sem.at[11], recv_sem=sib_sem.at[i],
            device_id=(r, 2 * q + (1 - k)), device_id_type=MESH,
        ).start()
    for i, group in enumerate(groups):
        mine = trail(group, k)
        pltpu.make_async_copy(sib_r.at[i], sib_r.at[i], sib_sem.at[i]).wait()
        mine = mine + sib_r[i]
        for j, o in enumerate(group):
            slot = 4 * o[0] + o[1]
            if slot:
                trail_s[slot] = mine[32 * j:32 * (j + 1)]
                remote(trail_s.at[slot], trail_r.at[slot], 12, r, 2 * chip(o) + k)
            else:
                trail_r[0] = mine[32 * j:32 * (j + 1)]
    sent(second_z.at[pl.ds(0, 15)], 10)
    sent(sib_s, 11)
    received(trail_r.at[pl.ds(0, 15)], 12)
    share_ref[...] = tree_sum(trail_r[i] for i in range(16))
    sent(trail_s.at[pl.ds(0, 15)], 12)


def on_device(*args):
    left, prior, diag, inverse, sub, panel, rhs = args
    tiles = lambda n: pltpu.VMEM((n, 8, 128), F32)
    left, prior, diag, inverse, sub, panel = (pltpu.with_memory_space_constraint(a, pltpu.HBM) for a in (left, prior, diag, inverse, sub, panel))
    solved, share = pl.pallas_call(
        kernel,
        out_shape=(jax.ShapeDtypeStruct((2, 64, 128), F32), jax.ShapeDtypeStruct((32, 128), F32)),
        in_specs=[pl.BlockSpec(memory_space=pltpu.HBM)] * 6,
        out_specs=(pl.BlockSpec(memory_space=pltpu.VMEM), pl.BlockSpec(memory_space=pltpu.VMEM)),
        scratch_shapes=[
            pltpu.VMEM((2, 128, 2048), F32),
            pltpu.VMEM((2048, 128), F32),
            pltpu.VMEM((128, 128), F32),
            pltpu.VMEM((2, 64, 128), F32),
            pltpu.VMEM((WINDOW, 64, 128), F32),
            pltpu.VMEM((WINDOW, 64, 128), F32),
            pltpu.VMEM((2, 64, 1024), F32),
            pltpu.VMEM((2048, 256), BF16),
            tiles(16),
            tiles(16),
            tiles(16),
            tiles(32),
            tiles(32),
            tiles(16),
            pltpu.VMEM((8, 128), F32),
            pltpu.VMEM((8, 128), F32),
            pltpu.VMEM((256, 128), BF16),
            pltpu.VMEM((256, 128), BF16),
            tiles(8),
            tiles(16),
            tiles(8),
            pltpu.VMEM((64, 1024), BF16),
            pltpu.VMEM((64, 1024), BF16),
            tiles(16),
            tiles(32),
            tiles(16),
            pltpu.VMEM((1024, 128), BF16),
            tiles(16),
            pltpu.VMEM((32, 32, 256), BF16),
            pltpu.VMEM((4, 128, 128), F32),
            pltpu.VMEM((4, 128, 128), F32),
            pltpu.VMEM((16, 32, 128), F32),
            pltpu.VMEM((16, 32, 128), F32),
            pltpu.SemaphoreType.DMA((5,)),
            pltpu.SemaphoreType.DMA((2, CHUNKS)),
            pltpu.SemaphoreType.DMA((17,)),
            pltpu.SemaphoreType.DMA((17,)),
            pltpu.SemaphoreType.DMA((4,)),
            pltpu.SemaphoreType.REGULAR,
        ],
        compiler_params=pltpu.CompilerParams(
            collective_id=0, has_side_effects=True, vmem_limit_bytes=32 * 1024 * 1024
        ),
    )(left, prior, diag, inverse, sub, panel)
    return solved, rhs - share


def solution(mesh):
    in_specs = (
        P(None, "row", "col"),
        P("col", None),
        P(None, "row", None),
        P(None, "col", "row"),
        P("col", "row"),
        P(None, "col", "row"),
        P(("row", "col"), None),
    )
    out_specs = (P(None, "col", None), P(("row", "col"), None))
    return jax.shard_map(
        on_device, mesh=mesh, in_specs=in_specs, out_specs=out_specs, check_vma=False
    )
```

```python
import jax
import jax.numpy as jnp
from jax import lax
from jax.experimental import pallas as pl
from jax.experimental.pallas import tpu as pltpu
from jax.sharding import PartitionSpec as P


F32 = jnp.float32
BF16 = jnp.bfloat16
MESH = pl.DeviceIdType.MESH
NZ = 16
CHUNKS = 2
WINDOW = 8
RED0, RED1, RES0, RES1, FIRST, UPDATE, GROUP, SOLVE, SECOND, TRAIL, PANEL, LOW0, ROWS, SUB, LOW = *range(13), 13, 15


def ring4(d):
    return min(d, 4 - d)


CHIPS = sorted(((dy, dx) for dy in range(4) for dx in range(4)), key=lambda o: (-(ring4(o[0]) + ring4(o[1])), o))
NEAR_Z = (2, 14, 1, 15)
FAR_Z = sorted(range(1, NZ), key=lambda d: -min(d, NZ - d))


def split(x):
    high = x.astype(BF16)
    return high, (x - high.astype(F32)).astype(BF16)


def dot(a, b):
    return jnp.dot(a, b, preferred_element_type=F32)


def tree_sum(terms):
    terms = list(terms)
    while len(terms) > 1:
        paired = [terms[i] + terms[i + 1] for i in range(0, len(terms) - 1, 2)]
        if len(terms) % 2:
            paired.append(terms[-1])
        terms = paired
    return terms[0]


def kernel(
    left, prior, diag, inverse, sub, panel, solved_ref, share_ref,
    left_v, prior_v, diag_v, inverse_v, sub_g, low_g, low0_v, panel_v,
    prior_w, diag_t, part0, part1, red0, red1, res0, res1, res1_in,
    first_s, first_z, first_o, first_g, sub_h, sub_l, upd_s, upd_r, x_t, low1_w, second_s, second_z,
    panel_w, rows_s, rows_r, trail_s, trail_r,
    load_sem, chunk_sem, send_sem, recv_sem, passed_sem,
):
    r = lax.axis_index("row")
    c = lax.axis_index("col")
    y, x, k = c // 8, (c // 2) % 4, c % 2
    q = c // 2
    ys = [(y + d) % 4 for d in range(4)]
    xs = [(x + d) % 4 for d in range(4)]
    zs = [(r + d) % NZ for d in range(NZ)]
    group = r % 8
    half = group // 4
    mine = pl.ds(pl.multiple_of(64 * k, 64), 64)
    theirs = pl.ds(pl.multiple_of(64 * (1 - k), 64), 64)
    other = 2 * q + (1 - k)

    def chip(o):
        return ys[o[0]] * 4 + xs[o[1]]

    ahead = (r - q // 2 + 4 + NZ) % NZ
    dst_row = q // 2 + 8 * (ahead // 8)
    dst_chip = 2 * (ahead % 8) + q % 2
    away = jnp.logical_or(dst_row != r, dst_chip != q)

    step = prior.shape[0] // CHUNKS
    for i in range(CHUNKS):
        rows = pl.ds(i * step, step)
        pltpu.make_async_copy(prior.at[rows, :], prior_v.at[rows, :], chunk_sem.at[0, i]).start()
        pltpu.make_async_copy(left.at[0, :, rows], left_v.at[0, :, rows], chunk_sem.at[1, i]).start()
    loads = [
        pltpu.make_async_copy(left.at[1], left_v.at[1], load_sem.at[0]),
        pltpu.make_async_copy(diag, diag_v, load_sem.at[1]),
        pltpu.make_async_copy(inverse, inverse_v, load_sem.at[2]),
        pltpu.make_async_copy(sub, sub_g.at[4, mine], load_sem.at[3]),
        pltpu.make_async_copy(panel, panel_v.at[k], load_sem.at[4]),
    ]

    barrier = pltpu.get_barrier_semaphore()

    def greet(row, col):
        pl.semaphore_signal(barrier, inc=1, device_id=(row, col), device_id_type=MESH)

    @pl.when(k == 0)
    def _():
        for o in CHIPS:
            greet(r, 2 * chip(o) + 1)
            if o != (0, 0):
                greet(r, 2 * chip(o))
        for d in NEAR_Z:
            greet(zs[d], c)
            greet(zs[d], c + 1)

    @pl.when(k == 1)
    def _():
        greet(r, c - 1)

    for copy in loads:
        copy.start()

    def remote(src, dst, number, row, col):
        pltpu.make_async_remote_copy(
            src_ref=src, dst_ref=dst, send_sem=send_sem.at[number], recv_sem=recv_sem.at[number],
            device_id=(row, col), device_id_type=MESH,
        ).start()

    def received(tiles, number):
        size = prior_v.at[pl.ds(0, 8 * tiles)]
        pltpu.make_async_copy(size, size, recv_sem.at[number]).wait()

    def sent(tiles, number):
        size = prior_v.at[pl.ds(0, 8 * tiles)]
        pltpu.make_async_copy(size, size, send_sem.at[number]).wait()

    def to_reducers(src, dst, number, both):
        for o in CHIPS[:-1]:
            slot = 4 * o[0] + o[1]
            remote(src.at[chip(o)], dst.at[2 * slot + k if both else slot], number, r, 2 * chip(o))
        if both:

            @pl.when(k == 1)
            def _():
                remote(src.at[q], dst.at[1], number, r, 2 * q)

        @pl.when(k == 0)
        def _():
            dst[0] = src[q]

    def from_reducer(ref, number):
        for o in CHIPS[:-1]:
            remote(ref.at[q], ref.at[q], number, r, 2 * chip(o))

    def window_start(ref, number):
        for w in (2, 6, 3, 5):
            remote(ref.at[4, mine], ref.at[w, mine], number, zs[(4 - w) % NZ], 2 * q)

        @pl.when(k == 1)
        def _():
            remote(ref.at[4, mine], ref.at[4, mine], number, r, 2 * q)

    def window_hand_on(ref, number):
        received(72, number)
        remote(ref.at[2], ref.at[0], number + 1, zs[2], c)
        remote(ref.at[2], ref.at[1], number + 1, zs[1], c)
        remote(ref.at[6], ref.at[7], number + 1, zs[15], c)

    def left_product(b):
        total = None
        for i in range(CHUNKS):
            rows = pl.ds(i * step, step)
            if b == 0:
                pltpu.make_async_copy(prior.at[rows, :], prior_v.at[rows, :], chunk_sem.at[0, i]).wait()
                prior_w[rows, :] = jnp.concatenate(split(prior_v[rows, :]), axis=1)
                pltpu.make_async_copy(left.at[0, :, rows], left_v.at[0, :, rows], chunk_sem.at[1, i]).wait()
            wide = dot(jnp.concatenate(split(left_v[b, :, rows]), axis=0), prior_w[rows, :])
            total = wide if total is None else total + wide
        return chunks(total[:128, :128] + total[:128, 128:] + total[128:, :128])

    def chunks(product):
        return product.T.reshape(16, 8, 128)

    part0[...] = left_product(0)

    pl.semaphore_wait(barrier, 20)

    to_reducers(part0, red0, RED0, True)

    def pass_on(number, distance):
        for d in (distance, NZ - distance):
            pl.semaphore_signal(passed_sem.at[number], inc=1, device_id=(zs[d], c), device_id_type=MESH)

    @pl.when(k == 0)
    def _():
        pass_on(0, 2)

    loads[3].wait()
    window_start(sub_g, SUB)
    loads[2].wait()
    row_ids = c * 64 + lax.broadcasted_iota(jnp.int32, (64, 128), 0)
    col_ids = r * 128 + lax.broadcasted_iota(jnp.int32, (64, 128), 1)
    keep = row_ids >= col_ids
    low_g[4, mine] = jnp.where(keep, inverse_v[1], 0.0)
    window_start(low_g, LOW)
    low0_v[mine] = jnp.where(keep, inverse_v[0], 0.0)

    @pl.when(k == 1)
    def _():
        remote(low0_v.at[mine], low0_v.at[mine], LOW0, r, other)

    loads[0].wait()
    part1[...] = left_product(1)
    to_reducers(part1, red1, RED1, True)
    loads[4].wait()
    remote(panel_v.at[k], panel_v.at[k], PANEL, r, other)
    loads[1].wait()

    @pl.when(k == 0)
    def _():
        for b in range(2):
            diag_t[b] = chunks(diag_v[b])
        pl.semaphore_wait(passed_sem.at[0], 2)
        pass_on(1, 4)
        received(31, RED0)
        res0[q] = diag_t[0, q] - tree_sum(red0[i] for i in range(32))
        from_reducer(res0, RES0)
        received(8, LOW0)
        high, low = split(low0_v[...].T)
        window_hand_on(sub_g, SUB)
        window_hand_on(low_g, LOW)
        received(15, RES0)

        res_h, res_l = split(jnp.concatenate([res0[i] for i in range(16)], axis=0))
        both = dot(jnp.concatenate([res_h, res_l], axis=0), high)
        first_s[...] = (both[:128] + both[128:] + dot(res_h, low)).reshape(8, 2, 8, 128)
        pl.semaphore_wait(passed_sem.at[1], 2)
        for d in FAR_Z:
            remote(first_s.at[zs[d] % 8], first_z.at[d], FIRST, zs[d], c)

        received(48, SUB + 1)
        received(48, LOW + 1)
        received(31, RED1)
        chunk = diag_t[1, q] - tree_sum(red1[i] for i in range(32))

        @pl.when(away)
        def _():
            res1[...] = chunk
            remote(res1, res1_in, RES1, dst_row, 2 * dst_chip)

        @pl.when(jnp.logical_not(away))
        def _():
            res1_in[...] = chunk

        for w in range(WINDOW):
            high, low = split(sub_g[w])
            sub_h[:, 128 * w:128 * (w + 1)] = high
            sub_l[:, 128 * w:128 * (w + 1)] = low
        for w in range(WINDOW):
            low1_w[128 * w:128 * (w + 1), :] = jnp.concatenate(split(low_g[w].T), axis=1)

    received(128, PANEL)
    for i in range(8):
        highs, lows = [], []
        for b in range(2):
            cols = slice(128 * i, 128 * (i + 1))
            high, low = split(jnp.concatenate([panel_v[0, b, :, cols], panel_v[1, b, :, cols]], axis=0).T)
            highs.append(high)
            lows.append(low)
        panel_w[4 * i:4 * (i + 1)] = jnp.concatenate(highs + lows, axis=1).reshape(4, 32, 512)

    @pl.when(k == 0)
    def _():
        received(30, FIRST)
        first = first_s[group] + tree_sum(first_z[d] for d in range(1, NZ))
        place = pl.ds(2 * (group % 4), 2)
        first_o[...] = first

        high, low = split(first.reshape(16, 128))
        both = dot(jnp.concatenate([high, low], axis=0), sub_h[...])
        update = both[:16] + both[16:] + dot(high, sub_l[...])
        for w in range(WINDOW):
            for h in range(2):
                upd_s[2 * w + h] = update[8 * h:8 * (h + 1), 128 * w:128 * (w + 1)]
        to_reducers(upd_s, upd_r, UPDATE, False)

        for w in (0, 1, 7, 2, 6, 3, 5):
            remote(first_o, first_g.at[place], GROUP, zs[(4 - w) % NZ], 2 * q + half)

        @pl.when(half == 1)
        def _():
            remote(first_o, first_g.at[place], GROUP, r, c + 1)

        @pl.when(half == 0)
        def _():
            first_g[place] = first

        @pl.when(away)
        def _():
            sent(1, RES1)
            received(1, RES1)

        received(15, UPDATE)
        x_t[q] = res1_in[...] - tree_sum(upd_r[i] for i in range(16))
        from_reducer(x_t, SOLVE)
        sent(15, RED0)
        sent(15, RED1)
        sent(15, RES0)
        sent(30, FIRST)
        sent(32, SUB)
        sent(48, SUB + 1)
        sent(32, LOW)
        sent(48, LOW + 1)
        received(15, SOLVE)

        upper = jnp.concatenate([x_t[2 * w] for w in range(WINDOW)], axis=1)
        under = jnp.concatenate([x_t[2 * w + 1] for w in range(WINDOW)], axis=1)
        high, low = split(jnp.concatenate([upper, under], axis=0))
        both = dot(jnp.concatenate([high, low], axis=0), low1_w[...])
        second = (both[:16, :128] + both[16:, :128] + both[:16, 128:]).reshape(2, 8, 128)
        second_s[...] = second
        place = pl.ds(8 * (r // 8) + 2 * (group % 4), 2)
        for d in FAR_Z:
            remote(second_s, second_z.at[place], SECOND, zs[d], 2 * q + half)

        @pl.when(half == 1)
        def _():
            remote(second_s, second_z.at[place], SECOND, r, c + 1)
            sent(16, GROUP)
            sent(32, SECOND)

        @pl.when(half == 0)
        def _():
            second_z[place] = second
            sent(14, GROUP)
            sent(30, SECOND)

        sent(15, UPDATE)
        sent(15, SOLVE)

    @pl.when(k == 1)
    def _():
        sent(16, RED0)
        sent(16, RED1)
        sent(40, SUB)
        sent(40, LOW)
        sent(8, LOW0)

    own = jnp.logical_and(k == 0, half == 0)

    @pl.when(own)
    def _():
        received(6, GROUP)
        received(14, SECOND)

    @pl.when(jnp.logical_not(own))
    def _():
        received(8, GROUP)
        received(16, SECOND)

    turned = jnp.concatenate(
        [first_g[i] for i in range(8)] + [second_z[i] + second_z[8 + i] for i in range(8)], axis=0
    ).T
    lane = lax.broadcasted_iota(jnp.int32, (128, 128), 1) < 64
    high = turned.astype(BF16).astype(F32)
    low = turned - high
    high_r, low_r = pltpu.roll(high, 64, 1), pltpu.roll(low, 64, 1)
    weights = jnp.concatenate(
        [
            jnp.where(lane, high, low_r), jnp.where(lane, high_r, low),
            jnp.where(lane, high, 0.0), jnp.where(lane, high_r, 0.0),
        ],
        axis=0,
    ).astype(BF16)

    packed_half = lax.broadcasted_iota(jnp.int32, (16, 128), 1) < 64
    for i in range(4):
        part = CHIPS[4 * i:4 * (i + 1)]
        lines = jnp.concatenate([panel_w[2 * chip(o) + e] for o in part for e in range(2)], axis=0)
        wide = dot(lines, weights)
        wide = (wide + pltpu.roll(wide, 64, 1)).reshape(8, 2, 16, 128)
        for j, o in enumerate(part):
            slot = 2 * (4 * o[0] + o[1])
            for e in range(2):
                packed = jnp.where(packed_half, wide[2 * j + e, 0], wide[2 * j + e, 1])
                trail_s[slot + e] = packed
                if slot:
                    remote(trail_s.at[slot + e], trail_r.at[slot + k], TRAIL, r, 2 * chip(o) + e)
    remote(trail_s.at[1 - k], trail_r.at[k], TRAIL, r, other)
    trail_r[k] = trail_s[k]

    rows_s[...] = turned
    remote(rows_s.at[theirs], rows_r, ROWS, r, other)
    narrow = lax.broadcasted_iota(jnp.int32, (64, 128), 1) < 64
    sent(128, PANEL)
    received(8, ROWS)
    here, there = rows_s[mine], rows_r[...]
    lower = jnp.where(k == 0, here, there)
    upper = jnp.where(k == 0, there, here)
    solved_ref[0] = jnp.where(narrow, lower, pltpu.roll(upper, 64, 1))
    solved_ref[1] = jnp.where(narrow, pltpu.roll(lower, 64, 1), upper)
    sent(8, ROWS)
    received(62, TRAIL)
    lower = tree_sum(trail_r[2 * i] for i in range(16))
    upper = tree_sum(trail_r[2 * i + 1] for i in range(16))
    share_ref[:16] = jnp.where(packed_half, lower, pltpu.roll(upper, 64, 1))
    share_ref[16:] = jnp.where(packed_half, pltpu.roll(lower, 64, 1), upper)
    sent(62, TRAIL)


def on_device(*args):
    left, prior, diag, inverse, sub, panel = (
        pltpu.with_memory_space_constraint(a, pltpu.HBM) for a in args[:6]
    )
    tiles = lambda *n: pltpu.VMEM((*n, 8, 128), F32)
    solved, share = pl.pallas_call(
        kernel,
        out_shape=(jax.ShapeDtypeStruct((2, 64, 128), F32), jax.ShapeDtypeStruct((32, 128), F32)),
        in_specs=[pl.BlockSpec(memory_space=pltpu.HBM)] * 6,
        out_specs=(pl.BlockSpec(memory_space=pltpu.VMEM), pl.BlockSpec(memory_space=pltpu.VMEM)),
        scratch_shapes=[
            pltpu.VMEM((2, 128, 2048), F32),
            pltpu.VMEM((2048, 128), F32),
            pltpu.VMEM((2, 128, 128), F32),
            pltpu.VMEM((2, 64, 128), F32),
            pltpu.VMEM((WINDOW, 128, 128), F32),
            pltpu.VMEM((WINDOW, 128, 128), F32),
            pltpu.VMEM((128, 128), F32),
            pltpu.VMEM((2, 2, 64, 1024), F32),
            pltpu.VMEM((2048, 256), BF16),
            tiles(2, 16),
            tiles(16),
            tiles(16),
            tiles(32),
            tiles(32),
            tiles(16),
            tiles(),
            tiles(),
            tiles(8, 2),
            tiles(16, 2),
            tiles(2),
            tiles(8),
            pltpu.VMEM((128, 1024), BF16),
            pltpu.VMEM((128, 1024), BF16),
            tiles(16),
            tiles(16),
            tiles(16),
            pltpu.VMEM((1024, 256), BF16),
            tiles(2),
            tiles(16),
            pltpu.VMEM((32, 32, 512), BF16),
            pltpu.VMEM((128, 128), F32),
            pltpu.VMEM((64, 128), F32),
            pltpu.VMEM((32, 16, 128), F32),
            pltpu.VMEM((32, 16, 128), F32),
            pltpu.SemaphoreType.DMA((5,)),
            pltpu.SemaphoreType.DMA((2, CHUNKS)),
            pltpu.SemaphoreType.DMA((17,)),
            pltpu.SemaphoreType.DMA((17,)),
            pltpu.SemaphoreType.REGULAR((2,)),
        ],
        compiler_params=pltpu.CompilerParams(
            collective_id=0, has_side_effects=True, vmem_limit_bytes=32 * 1024 * 1024
        ),
    )(left, prior, diag, inverse, sub, panel)
    return solved, args[6] - share


def solution(mesh):
    in_specs = (
        P(None, "row", "col"),
        P("col", None),
        P(None, "row", None),
        P(None, "col", "row"),
        P("col", "row"),
        P(None, "col", "row"),
        P(("row", "col"), None),
    )
    out_specs = (P(None, "col", None), P(("row", "col"), None))
    return jax.shard_map(
        on_device, mesh=mesh, in_specs=in_specs, out_specs=out_specs, check_vma=False
    )
```

```python
import jax
import jax.numpy as jnp
from jax import lax
from jax.experimental import pallas as pl
from jax.experimental.pallas import tpu as pltpu
from jax.sharding import PartitionSpec as P


F32 = jnp.float32
BF16 = jnp.bfloat16
MESH = pl.DeviceIdType.MESH
NZ = 16
CHUNKS = 2
WINDOW = 8
SUB, LOW = 13, 15


def ring4(d):
    return min(d, 4 - d)


CHIPS = sorted(((dy, dx) for dy in range(4) for dx in range(4)), key=lambda o: (-(ring4(o[0]) + ring4(o[1])), o))
NEAR_Z = (4, 12, 3, 13, 2, 14, 1, 15)
FAR_Z = sorted(range(1, NZ), key=lambda d: -min(d, NZ - d))


def split(x):
    high = x.astype(BF16)
    return high, (x - high.astype(F32)).astype(BF16)


def dot(a, b):
    return jnp.dot(a, b, preferred_element_type=F32)


def tree_sum(terms):
    terms = list(terms)
    while len(terms) > 1:
        paired = [terms[i] + terms[i + 1] for i in range(0, len(terms) - 1, 2)]
        if len(terms) % 2:
            paired.append(terms[-1])
        terms = paired
    return terms[0]


def kernel(
    left, prior, diag, inverse, sub, panel, solved_ref, share_ref,
    left_v, prior_v, diag_v, inverse_v, sub_g, low_g, panel_v,
    prior_w, diag_t, part0, part1, red0, red1, res0, res1, res1_in, low0_h, low0_l,
    first_s, first_z, first_g, sub_h, sub_l, upd_s, upd_r, x_t, low1_w, second_z,
    panel_w, sib_s, sib_r, trail_s, trail_r,
    load_sem, chunk_sem, send_sem, recv_sem, sib_sem, passed_sem,
):
    r = lax.axis_index("row")
    c = lax.axis_index("col")
    y, x, k = c // 8, (c // 2) % 4, c % 2
    q = c // 2
    ys = [(y + d) % 4 for d in range(4)]
    xs = [(x + d) % 4 for d in range(4)]
    zs = [(r + d) % NZ for d in range(NZ)]

    def chip(o):
        return ys[o[0]] * 4 + xs[o[1]]

    ahead = (r - q // 2 + 4 + NZ) % NZ
    dst_row = q // 2 + 8 * (ahead // 8)
    dst_chip = 2 * (ahead % 8) + q % 2
    away = jnp.logical_or(dst_row != r, dst_chip != q)

    step = prior.shape[0] // CHUNKS
    for i in range(CHUNKS):
        rows = pl.ds(i * step, step)
        pltpu.make_async_copy(prior.at[rows, :], prior_v.at[rows, :], chunk_sem.at[0, i]).start()
        pltpu.make_async_copy(left.at[0, :, rows], left_v.at[0, :, rows], chunk_sem.at[1, i]).start()
    loads = [
        pltpu.make_async_copy(left.at[1], left_v.at[1], load_sem.at[0]),
        pltpu.make_async_copy(diag.at[k], diag_v, load_sem.at[1]),
        pltpu.make_async_copy(inverse, inverse_v, load_sem.at[2]),
        pltpu.make_async_copy(sub, sub_g.at[4], load_sem.at[3]),
        pltpu.make_async_copy(panel, panel_v, load_sem.at[4]),
    ]

    barrier = pltpu.get_barrier_semaphore()

    def greet(row, col):
        pl.semaphore_signal(barrier, inc=1, device_id=(row, col), device_id_type=MESH)

    for o in CHIPS[:5]:
        greet(r, 2 * chip(o) + (1 - k))
        greet(r, 2 * chip(o) + k)
    for d in NEAR_Z:
        greet(zs[d], c)
    for o in CHIPS[5:]:
        greet(r, 2 * chip(o) + (1 - k))
        if o != (0, 0):
            greet(r, 2 * chip(o) + k)
    for copy in loads:
        copy.start()

    def remote(src, dst, number, row, col):
        pltpu.make_async_remote_copy(
            src_ref=src, dst_ref=dst, send_sem=send_sem.at[number], recv_sem=recv_sem.at[number],
            device_id=(row, col), device_id_type=MESH,
        ).start()

    def received(ref, number):
        pltpu.make_async_copy(ref, ref, recv_sem.at[number]).wait()

    def sent(ref, number):
        pltpu.make_async_copy(ref, ref, send_sem.at[number]).wait()

    def to_reducers(src, dst, core, number):
        for o in CHIPS[:-1]:
            remote(src.at[chip(o)], dst.at[2 * (4 * o[0] + o[1]) + k], number, r, 2 * chip(o) + core)

        @pl.when(k != core)
        def _():
            remote(src.at[q], dst.at[k], number, r, 2 * q + core)

        @pl.when(k == core)
        def _():
            dst[core] = src[q]

    def to_reducers_sent(ref, core, number):
        @pl.when(k == core)
        def _():
            sent(ref.at[pl.ds(0, 15)], number)

        @pl.when(k != core)
        def _():
            sent(ref, number)

    def from_reducer(ref, core, number):
        for o in CHIPS:
            remote(ref.at[q], ref.at[q], number, r, 2 * chip(o) + (1 - core))
            if o != (0, 0):
                remote(ref.at[q], ref.at[q], number, r, 2 * chip(o) + core)

    def from_reducers_received(ref, core, number):
        @pl.when(k == core)
        def _():
            received(ref.at[pl.ds(0, 15)], number)

        @pl.when(k != core)
        def _():
            received(ref, number)

    def window_start(ref, number):
        for w in (2, 6, 3, 5):
            remote(ref.at[4], ref.at[w], number, zs[(4 - w) % NZ], c)

    def window_hand_on(ref, number):
        received(ref.at[pl.ds(0, 4)], number)
        remote(ref.at[2], ref.at[0], number + 1, zs[2], c)
        remote(ref.at[2], ref.at[1], number + 1, zs[1], c)
        remote(ref.at[6], ref.at[7], number + 1, zs[15], c)

    def window_end(ref, number):
        received(ref.at[pl.ds(0, 3)], number + 1)
        sent(ref.at[pl.ds(0, 4)], number)
        sent(ref.at[pl.ds(0, 3)], number + 1)

    def left_product(b, parts):
        total = None
        for i in parts:
            rows = pl.ds(i * step, step)
            if b == 0:
                pltpu.make_async_copy(prior.at[rows, :], prior_v.at[rows, :], chunk_sem.at[0, i]).wait()
                prior_w[rows, :] = jnp.concatenate(split(prior_v[rows, :]), axis=1)
                pltpu.make_async_copy(left.at[0, :, rows], left_v.at[0, :, rows], chunk_sem.at[1, i]).wait()
            wide = dot(jnp.concatenate(split(left_v[b, :, rows]), axis=0), prior_w[rows, :])
            total = wide if total is None else total + wide
        return total[:128, :128] + total[:128, 128:] + total[128:, :128]

    def chunks(product):
        return product.T.reshape(16, 8, 128)

    part0[...] = chunks(left_product(0, range(CHUNKS)))

    pl.semaphore_wait(barrier, 39)

    to_reducers(part0, red0, 0, 0)
    for d in NEAR_Z:
        pl.semaphore_signal(passed_sem, inc=1, device_id=(zs[d], c), device_id_type=MESH)

    loads[3].wait()
    window_start(sub_g, SUB)
    loads[2].wait()
    row_ids = c * 64 + lax.broadcasted_iota(jnp.int32, (64, 128), 0)
    col_ids = r * 128 + lax.broadcasted_iota(jnp.int32, (64, 128), 1)
    keep = row_ids >= col_ids
    low_g[4] = jnp.where(keep, inverse_v[1], 0.0)
    window_start(low_g, LOW)
    loads[1].wait()
    diag_t[...] = diag_v[...].T.reshape(16, 8, 128)
    low0 = jnp.where(keep, inverse_v[0], 0.0)
    nothing = jnp.zeros((64, 128), F32)
    high, low = split(
        jnp.concatenate(
            [jnp.concatenate([low0, nothing], axis=1), jnp.concatenate([nothing, low0], axis=1)], axis=0
        ).T
    )
    low0_h[...] = high
    low0_l[...] = low

    loads[0].wait()
    diag_v[...] = left_product(1, range(CHUNKS // 2))

    @pl.when(k == 0)
    def _():
        received(red0.at[pl.ds(0, 31)], 0)
        res0[q] = diag_t[q] - tree_sum(red0[i] for i in range(32))
        from_reducer(res0, 0, 2)

    part1[...] = chunks(diag_v[...] + left_product(1, range(CHUNKS // 2, CHUNKS)))
    to_reducers(part1, red1, 1, 1)
    window_hand_on(sub_g, SUB)
    window_hand_on(low_g, LOW)
    to_reducers_sent(part0, 0, 0)
    from_reducers_received(res0, 0, 2)

    even = jnp.concatenate([res0[2 * i] for i in range(8)], axis=0)
    odd = jnp.concatenate([res0[2 * i + 1] for i in range(8)], axis=0)
    high, low = split(jnp.concatenate([even, odd], axis=1))
    both = dot(jnp.concatenate([high, low], axis=0), low0_h[...])
    first_s[...] = (both[:64] + both[64:] + dot(high, low0_l[...])).reshape(8, 8, 128)
    pl.semaphore_wait(passed_sem, 8)
    for d in FAR_Z:
        remote(first_s.at[zs[d] % 8], first_z.at[d], 5, zs[d], c)
    group = r % 8

    loads[4].wait()
    for i in range(8):
        block = panel_v[:, :, 128 * i:128 * (i + 1)].reshape(128, 128).T
        panel_w[4 * i:4 * (i + 1)] = jnp.concatenate(split(block), axis=1).reshape(4, 32, 256)
    window_end(sub_g, SUB)
    for w in range(WINDOW):
        high, low = split(sub_g[w])
        sub_h[:, 128 * w:128 * (w + 1)] = high
        sub_l[:, 128 * w:128 * (w + 1)] = low
    window_end(low_g, LOW)
    for w in range(WINDOW):
        high, low = split(low_g[w])
        stacked = jnp.concatenate([high.astype(F32), low.astype(F32)], axis=0).T
        low1_w[128 * w:128 * (w + 1), :] = stacked.astype(BF16)

    @pl.when(k == 1)
    def _():
        received(red1.at[pl.ds(0, 31)], 1)
        mine = diag_t[q] - tree_sum(red1[i] for i in range(32))

        @pl.when(away)
        def _():
            res1[...] = mine
            remote(res1, res1_in, 3, dst_row, 2 * dst_chip + 1)

        @pl.when(jnp.logical_not(away))
        def _():
            res1_in[...] = mine

    to_reducers_sent(part1, 1, 1)

    @pl.when(k == 0)
    def _():
        sent(red0.at[pl.ds(0, 31)], 2)

    received(first_z.at[pl.ds(0, 15)], 5)
    first = first_s[group] + tree_sum(first_z[d] for d in range(1, NZ))
    first_g[group] = first

    high, low = split(jnp.concatenate([first[:, :64], first[:, 64:]], axis=0))
    both = dot(jnp.concatenate([high, low], axis=0), sub_h[...])
    update = both[:16] + both[16:] + dot(high, sub_l[...])
    for w in range(WINDOW):
        for h in range(2):
            upd_s[2 * w + h] = update[8 * h:8 * (h + 1), 128 * w:128 * (w + 1)]
    to_reducers(upd_s, upd_r, 1, 7)

    for w in (0, 1, 7, 2, 6, 3, 5):
        remote(first_g.at[group], first_g.at[group], 8, zs[(4 - w) % NZ], c)
    sent(first_z.at[pl.ds(0, 15)], 5)

    @pl.when(k == 1)
    def _():
        @pl.when(away)
        def _():
            sent(res1, 3)
            received(res1_in, 3)

        received(upd_r.at[pl.ds(0, 31)], 7)
        x_t[q] = res1_in[...] - tree_sum(upd_r[i] for i in range(32))
        from_reducer(x_t, 1, 9)

    to_reducers_sent(upd_s, 1, 7)
    received(first_g.at[pl.ds(0, 7)], 8)
    sent(first_g.at[pl.ds(0, 7)], 8)
    from_reducers_received(x_t, 1, 9)

    upper = jnp.concatenate([x_t[2 * w] for w in range(WINDOW)], axis=1)
    under = jnp.concatenate([x_t[2 * w + 1] for w in range(WINDOW)], axis=1)
    high, low = split(jnp.concatenate([upper, under], axis=0))
    both = dot(jnp.concatenate([high, low], axis=0), low1_w[...])
    both = both[:16] + both[16:]
    both = both + pltpu.roll(both, 64, 1)
    left_half = lax.broadcasted_iota(jnp.int32, (8, 128), 1) < 64
    second_z[r] = jnp.where(left_half, both[:8], both[8:])
    for d in FAR_Z:
        remote(second_z.at[r], second_z.at[r], 10, zs[d], c)

    @pl.when(k == 1)
    def _():
        sent(upd_r.at[pl.ds(0, 31)], 9)

    received(second_z.at[pl.ds(0, 15)], 10)
    rows = []
    for g in range(8):
        a = first_g[g]
        b = second_z[g] + second_z[g + 8]
        rows.append(jnp.where(left_half, a, pltpu.roll(b, 64, 1)))
        rows.append(jnp.where(left_half, pltpu.roll(a, 64, 1), b))
    solved = jnp.concatenate(rows, axis=0).T
    solved_ref[...] = solved.reshape(2, 64, 128)

    high, low = split(solved)
    weights = jnp.concatenate(
        [jnp.concatenate([high, low], axis=1), jnp.concatenate([high, jnp.zeros((128, 128), BF16)], axis=1)], axis=0
    )

    def trail(group, core):
        lines = jnp.concatenate([panel_w[2 * chip(o) + core] for o in group], axis=0)
        wide = dot(lines, weights)
        return wide[:, :128] + wide[:, 128:]

    groups = [CHIPS[4 * i:4 * (i + 1)] for i in range(4)]
    for i, group in enumerate(groups):
        sib_s[i] = trail(group, 1 - k)
        pltpu.make_async_remote_copy(
            src_ref=sib_s.at[i], dst_ref=sib_r.at[i], send_sem=send_sem.at[11], recv_sem=sib_sem.at[i],
            device_id=(r, 2 * q + (1 - k)), device_id_type=MESH,
        ).start()
    for i, group in enumerate(groups):
        mine = trail(group, k)
        pltpu.make_async_copy(sib_r.at[i], sib_r.at[i], sib_sem.at[i]).wait()
        mine = mine + sib_r[i]
        for j, o in enumerate(group):
            slot = 4 * o[0] + o[1]
            if slot:
                trail_s[slot] = mine[32 * j:32 * (j + 1)]
                remote(trail_s.at[slot], trail_r.at[slot], 12, r, 2 * chip(o) + k)
            else:
                trail_r[0] = mine[32 * j:32 * (j + 1)]
    sent(second_z.at[pl.ds(0, 15)], 10)
    sent(sib_s, 11)
    received(trail_r.at[pl.ds(0, 15)], 12)
    share_ref[...] = tree_sum(trail_r[i] for i in range(16))
    sent(trail_s.at[pl.ds(0, 15)], 12)


def on_device(*args):
    left, prior, diag, inverse, sub, panel, rhs = args
    tiles = lambda n: pltpu.VMEM((n, 8, 128), F32)
    left, prior, diag, inverse, sub, panel = (pltpu.with_memory_space_constraint(a, pltpu.HBM) for a in (left, prior, diag, inverse, sub, panel))
    solved, share = pl.pallas_call(
        kernel,
        out_shape=(jax.ShapeDtypeStruct((2, 64, 128), F32), jax.ShapeDtypeStruct((32, 128), F32)),
        in_specs=[pl.BlockSpec(memory_space=pltpu.HBM)] * 6,
        out_specs=(pl.BlockSpec(memory_space=pltpu.VMEM), pl.BlockSpec(memory_space=pltpu.VMEM)),
        scratch_shapes=[
            pltpu.VMEM((2, 128, 2048), F32),
            pltpu.VMEM((2048, 128), F32),
            pltpu.VMEM((128, 128), F32),
            pltpu.VMEM((2, 64, 128), F32),
            pltpu.VMEM((WINDOW, 64, 128), F32),
            pltpu.VMEM((WINDOW, 64, 128), F32),
            pltpu.VMEM((2, 64, 1024), F32),
            pltpu.VMEM((2048, 256), BF16),
            tiles(16),
            tiles(16),
            tiles(16),
            tiles(32),
            tiles(32),
            tiles(16),
            pltpu.VMEM((8, 128), F32),
            pltpu.VMEM((8, 128), F32),
            pltpu.VMEM((256, 128), BF16),
            pltpu.VMEM((256, 128), BF16),
            tiles(8),
            tiles(16),
            tiles(8),
            pltpu.VMEM((64, 1024), BF16),
            pltpu.VMEM((64, 1024), BF16),
            tiles(16),
            tiles(32),
            tiles(16),
            pltpu.VMEM((1024, 128), BF16),
            tiles(16),
            pltpu.VMEM((32, 32, 256), BF16),
            pltpu.VMEM((4, 128, 128), F32),
            pltpu.VMEM((4, 128, 128), F32),
            pltpu.VMEM((16, 32, 128), F32),
            pltpu.VMEM((16, 32, 128), F32),
            pltpu.SemaphoreType.DMA((5,)),
            pltpu.SemaphoreType.DMA((2, CHUNKS)),
            pltpu.SemaphoreType.DMA((17,)),
            pltpu.SemaphoreType.DMA((17,)),
            pltpu.SemaphoreType.DMA((4,)),
            pltpu.SemaphoreType.REGULAR,
        ],
        compiler_params=pltpu.CompilerParams(
            collective_id=0, has_side_effects=True, vmem_limit_bytes=32 * 1024 * 1024
        ),
    )(left, prior, diag, inverse, sub, panel)
    return solved, rhs - share


def solution(mesh):
    in_specs = (
        P(None, "row", "col"),
        P("col", None),
        P(None, "row", None),
        P(None, "col", "row"),
        P("col", "row"),
        P(None, "col", "row"),
        P(("row", "col"), None),
    )
    out_specs = (P(None, "col", None), P(("row", "col"), None))
    return jax.shard_map(
        on_device, mesh=mesh, in_specs=in_specs, out_specs=out_specs, check_vma=False
    )
```
